256 devices in a mesh: row: 32 (over z, y_hi, core), col: 8 (over x, y_lo).
Axes of the slice: x: 4, y: 4 (y_hi: 2, y_lo: 2; y = y_hi * 2 + y_lo), z: 8, core: 2. Of those that a mesh axis runs over, the one named last changes fastest.
Arguments:
- gradient: bfloat16 [8192, 14336], P('row', 'col'), may hold values from -6 to 6
Outputs:
- statistics: float32 [8192, 8192], P(('row', 'col'))
The draws below stay inside these ranges and needn't reach their ends.
All inputs are finite; a program needn't handle non-finite values.
Results may differ from the reference program's by a relative error of at most 0.0003.
Values may be sent and summed in bfloat16 or wider, within the bound.
No kernel may reach another device: no remote copies, remote signals or barrier semaphores. Data moves between devices by JAX's collectives and lax.ppermute only.
A program may use at most 64 MiB of HBM per device.

```python
import jax
import jax.numpy as jnp
from jax import lax

M = 8192
NCOL = 14336


def raised(result, rng, source, target, shards_of, factor):
    def block_of(dim):
        return (jnp.arange(result.shape[dim]) // (result.shape[dim] // shards_of)).reshape((-1,) + (1,) * (result.ndim - 1 - dim))

    one_side = jax.random.permutation(rng, shards_of)[block_of(target)]
    far = (block_of(target) + shards_of // 2) % shards_of
    return jnp.where((block_of(source) == one_side) | (block_of(source) == far), factor * result, result)


def block_scale(own_key, extent, cuts, least, top_value):
    level, own = 1.0, jax.random.fold_in(own_key, 6)
    for axis_at, shards_of in cuts:
        draws = jnp.exp(jax.random.uniform(jax.random.fold_in(own, axis_at), (shards_of,), jnp.float32, least / len(cuts), top_value / len(cuts)))
        level = level * jnp.repeat(draws, extent[axis_at] // shards_of).reshape([-1 if axis == axis_at else 1 for axis in range(len(extent))])
    return level


def bell_draw_with(stream_key, shape, deviation, limit, split, heavy, dtype=jnp.bfloat16):
    drawn = deviation * jax.random.normal(stream_key, shape, jnp.float32)
    if split:
        drawn = drawn * block_scale(stream_key, shape, split, -0.22, 0.18)
    return jnp.clip(raised(drawn, jax.random.fold_in(stream_key, 3), *heavy), -limit, limit).astype(dtype)


def setup_inputs(seed: int = 0) -> dict:
    streams_of = jax.random.split(jax.random.key(seed), 2)
    return {
        "gradient": bell_draw_with(streams_of[0], (M, NCOL), 1.0, 6.0, ((0, 32), (1, 8)), (1, 0, 32, 2.75)),
    }


def reference(gradient):
    wide = gradient.astype(jnp.float32)
    total = jnp.dot(wide, wide.T, precision=lax.Precision.HIGHEST, preferred_element_type=jnp.float32)
    return total / NCOL
```

```python
import jax
import jax.numpy as jnp
import numpy as np
from jax import lax
from jax.experimental import pallas as pl
from jax.experimental.pallas import tpu as pltpu
from jax.sharding import PartitionSpec as P

NCOL = 14336
NZ = 8
AXES = ("row", "col")


def shift(value, dz=0, dy=0, dc=0):
    pairs = []
    for z in range(NZ):
        for y in range(2):
            for c in range(2):
                pairs.append(((z * 2 + y) * 2 + c, ((z + dz) % NZ * 2 + (y ^ dy)) * 2 + (c ^ dc)))
    return lax.ppermute(value, "row", pairs)


def product(left, right):
    return lax.dot_general(left, right, (((1,), (1,)), ((), ())), preferred_element_type=jnp.float32)


def arrange_kernel(where_ref, near_ref, far_ref, out_ref):
    width = out_ref.shape[1] // 32
    for block in range(32):
        place = where_ref[block]

        @pl.when(place < 20)
        def _():
            out_ref[:, block * width : (block + 1) * width] = near_ref[place] * (1.0 / NCOL)

        @pl.when(place >= 20)
        def _():
            out_ref[:, block * width : (block + 1) * width] = far_ref[place - 20] * (1.0 / NCOL)


def arrange(near, far, myself):
    z, mine = myself // 4, myself % 4
    block = jnp.arange(32)
    rel = (block % 4) ^ mine
    start = jnp.where(rel >= 2, 4, 0)
    at = (block // 4 - z - start) % 8
    where = jnp.where(at < 5, rel * 5 + at, 20 + rel * 3 + at - 5).astype(jnp.int32)
    rows, width = near.shape[1:]
    return pl.pallas_call(
        arrange_kernel,
        grid_spec=pltpu.PrefetchScalarGridSpec(
            num_scalar_prefetch=1,
            grid=(),
            in_specs=[pl.BlockSpec(memory_space=pltpu.VMEM)] * 2,
            out_specs=pl.BlockSpec(memory_space=pltpu.VMEM),
        ),
        out_shape=jax.ShapeDtypeStruct((rows, 32 * width), jnp.float32),
        compiler_params=pltpu.CompilerParams(vmem_limit_bytes=16 << 20),
    )(where, near, far)


def per_device(gradient):
    rows = gradient.shape[0]
    ncol = lax.axis_size("col")
    part = rows // ncol
    myself = lax.axis_index("row")

    above, below = shift(gradient, dz=-1), shift(gradient, dz=1)
    above, below = lax.optimization_barrier((above, below))
    above2, below2 = shift(above, dz=-1), shift(below, dz=1)
    above2, below2 = lax.optimization_barrier((above2, below2))
    other_y = shift(above2, dy=1)
    other_c = shift(below2, dc=1)
    other_x = shift(other_y, dc=1)

    window = jnp.concatenate([below2, below, gradient, above, above2], axis=0)
    sums = []
    for block in (below2, other_c, other_y, other_x):
        tiles = product(block, window).reshape(ncol, part, 5 * rows)
        sums.append(tiles)
    tiles = jnp.concatenate(sums, axis=2)
    tiles = lax.all_to_all(tiles, "col", 0, 0, tiled=True)
    total = tiles.sum(0).reshape(part, 4, 5, rows)

    home = [
        shift(total[:, 0], dz=-2),
        shift(total[:, 1], dz=-2, dc=1),
        shift(total[:, 2], dz=2, dy=1),
        shift(total[:, 3], dz=2, dy=1, dc=1),
    ]
    mirror = total[:, :, 1:4].reshape(part, 4, 3, ncol, part).transpose(3, 4, 2, 1, 0).reshape(ncol, part, 12 * part)
    mirror = lax.all_to_all(mirror, "col", 0, 0, tiled=True)
    mirror = mirror.reshape(ncol, part, 3, 4, part).transpose(2, 3, 1, 0, 4).reshape(3, 4, part, rows)
    far = [shift(mirror[2], dz=1), mirror[1], shift(mirror[0], dz=-1)]
    far = jnp.stack(far, axis=1).reshape(12, part, rows)
    near = jnp.stack(home, axis=0).transpose(0, 2, 1, 3).reshape(20, part, rows)
    return arrange(near, far, myself)


def solution(mesh):
    return jax.shard_map(
        per_device,
        mesh=mesh,
        in_specs=(P("row", "col"),),
        out_specs=P(("row", "col"), None),
        check_vma=False,
    )
```

```python
import jax
import jax.numpy as jnp
from jax import lax
from jax.experimental import pallas as pl
from jax.experimental.pallas import tpu as pltpu
from jax.sharding import PartitionSpec as P

NCOL = 14336
NZ = 8
LIMIT = 60000.0
LANES = 128
VMEM = pl.BlockSpec(memory_space=pltpu.VMEM)
ROOM = pltpu.CompilerParams(vmem_limit_bytes=16 << 20)


def shift(value, dz=0, dy=0, dc=0):
    pairs = []
    for z in range(NZ):
        for y in range(2):
            for c in range(2):
                pairs.append(((z * 2 + y) * 2 + c, ((z + dz) % NZ * 2 + (y ^ dy)) * 2 + (c ^ dc)))
    return lax.ppermute(value, "row", pairs)


def hold(value, *until):
    for other in until:
        corner = other[(slice(0, 1),) * other.ndim].reshape(1, 1)
        value = value + (corner * 0).astype(value.dtype)
    return value


def tiles_kernel(nrows, ncols, pairs, scaled, *refs):
    lefts, rights, out_ref = refs[:nrows], refs[nrows : nrows + ncols], refs[-1]
    ndest, part, full = out_ref.shape
    width = rights[0].shape[0]
    most = None
    for at, (left, right) in enumerate(pairs):
        tile = lax.dot_general(
            lefts[left][...], rights[right][...], (((1,), (1,)), ((), ())), preferred_element_type=jnp.float32
        )
        out_ref[:, :, at * width : (at + 1) * width] = tile.reshape(ndest, part, width)
        most = jnp.abs(tile) if most is None else jnp.maximum(most, jnp.abs(tile))
    if scaled:
        most = jnp.max(jnp.max(most, axis=0, keepdims=True), axis=1, keepdims=True)
        power = jnp.floor(jnp.log2(LIMIT / jnp.maximum(most, 1e-33)))
        factor = jnp.exp2(power) / (1.0 + lax.axis_index("col").astype(jnp.float32) / ndest)
        for at in range(len(pairs)):
            cut = slice(at * width, (at + 1) * width)
            out_ref[:, :, cut] = out_ref[:, :, cut] * factor.reshape(1, 1, 1)
        out_ref[:, :, full - LANES :] = jnp.broadcast_to(power.reshape(1, 1, 1), (ndest, part, LANES))


def tiles(lefts, rights, pairs, ndest, scaled=False):
    rows, depth = lefts[0].shape
    width = rows * len(pairs)
    return pl.pallas_call(
        lambda *refs: tiles_kernel(len(lefts), len(rights), pairs, scaled, *refs),
        in_specs=[VMEM] * (len(lefts) + len(rights)),
        out_specs=VMEM,
        out_shape=jax.ShapeDtypeStruct((ndest, rows // ndest, width + scaled * LANES), jnp.float32),
        compiler_params=ROOM,
        cost_estimate=pl.CostEstimate(
            flops=2 * rows * width * depth,
            bytes_accessed=2 * rows * depth * (len(lefts) + len(rights)) + 4 * rows * width,
            transcendentals=0,
        ),
    )(*lefts, *rights)


def turn_kernel(first_ref, second_ref, own_ref, core_ref, half_ref, cross_ref, out_ref):
    ndest, part, _ = out_ref.shape
    width = ndest * part

    def summed(ref):
        full = ref.shape[2]
        powers = [ref[source, :, full - LANES : full - LANES + 1] for source in range(ndest)]
        weights = [jnp.exp2(-power) * (1.0 + source / ndest) for source, power in enumerate(powers)]

        def total(at):
            cut = slice(at * width, (at + 1) * width)
            value = ref[0, :, cut] * weights[0]
            for source in range(1, ndest):
                value += ref[source, :, cut] * weights[source]
            return value

        return [total(at) for at in range(full // width)]

    first, second = summed(first_ref), summed(second_ref)
    for ref, blocks in (
        (own_ref, first[:3] + second[:1]),
        (core_ref, first[3:] + second[1:2]),
        (half_ref, second[2:6]),
        (cross_ref, second[6:]),
    ):
        for at, block in enumerate(blocks):
            ref[:, at * width : (at + 1) * width] = block
    groups = (
        (first[1], first[4], second[3], second[7]),
        (first[2], first[5], second[4], second[8]),
        (second[0], second[1], second[5], second[9]),
    )
    step = 4 * part
    for at, group in enumerate(groups):
        turned = jnp.concatenate(group, axis=0).T
        out_ref[:, :, at * step : (at + 1) * step] = turned.reshape(ndest, part, step)


def turn(first, second):
    ndest, part, _ = first.shape
    width = ndest * part
    bundle = jax.ShapeDtypeStruct((part, 4 * width), jnp.float32)
    return pl.pallas_call(
        turn_kernel,
        in_specs=[VMEM] * 2,
        out_specs=[VMEM] * 5,
        out_shape=[bundle] * 4 + [jax.ShapeDtypeStruct((ndest, part, 12 * part), jnp.float32)],
        compiler_params=ROOM,
    )(first, second)


def settle_kernel(in_ref, *outs):
    nsource, part, _ = in_ref.shape
    width = nsource * part
    place = 0
    for ref in outs:
        for at in range(ref.shape[1] // width):
            pieces = [in_ref[source, :, place * part : (place + 1) * part] for source in range(nsource)]
            ref[:, at * width : (at + 1) * width] = jnp.concatenate(pieces, axis=1)
            place += 1


def settle(turned):
    nsource, part, _ = turned.shape
    width = nsource * part
    return pl.pallas_call(
        settle_kernel,
        in_specs=[VMEM],
        out_specs=[VMEM] * 5,
        out_shape=[jax.ShapeDtypeStruct((part, count * width), jnp.float32) for count in (4, 2, 2, 2, 2)],
        compiler_params=ROOM,
    )(turned)


def arrange_kernel(to_ref, *refs):
    blocks, out_ref = refs[:-1], refs[-1]
    place = 0
    width = out_ref.shape[1] // 32
    for ref in blocks:
        for at in range(ref.shape[1] // width):
            start = pl.multiple_of(to_ref[place] * width, width)
            out_ref[:, pl.ds(start, width)] = ref[:, at * width : (at + 1) * width] * (1.0 / NCOL)
            place += 1


def arrange(blocks, labels, myself, rows, width):
    z, mine = myself // 4, myself % 4
    rel = jnp.array([k for k, _ in labels], jnp.int32)
    slab = jnp.array([d for _, d in labels], jnp.int32)
    to = ((z + slab) % NZ * 4 + (rel ^ mine)).astype(jnp.int32)
    return pl.pallas_call(
        arrange_kernel,
        grid_spec=pltpu.PrefetchScalarGridSpec(
            num_scalar_prefetch=1, grid=(), in_specs=[VMEM] * len(blocks), out_specs=VMEM
        ),
        out_shape=jax.ShapeDtypeStruct((rows, 32 * width), jnp.float32),
        compiler_params=ROOM,
    )(to, *blocks)


def per_device(gradient):
    rows = gradient.shape[0]
    ncol = lax.axis_size("col")
    part = rows // ncol
    myself = lax.axis_index("row")

    def exchange(parts):
        return lax.all_to_all(parts, "col", 0, 0, tiled=True)

    up1, down1 = shift(gradient, dz=-1), shift(gradient, dz=1)
    half1 = shift(up1, dy=1)
    core1 = shift(hold(down1, up1), dc=1)
    up2, down2 = shift(up1, dz=-1), shift(down1, dz=1)

    near = [(row, column) for row in range(2) for column in range(3)]
    first = tiles([down1, core1], [down1, gradient, up1], near, ncol, scaled=True)
    half1 = hold(half1, first)
    cross1 = shift(half1, dc=1)
    first = exchange(first.astype(jnp.float16))
    up3, down3 = shift(hold(up2, first), dz=-1), shift(hold(down2, first), dz=1)
    middle = [(0, 0), (1, 0)] + [(row, column) for row in (2, 3) for column in (1, 2, 3, 4)]
    second = tiles([down1, core1, half1, cross1], [up2, up1, gradient, down1, down2], middle, ncol, scaled=True)
    second = exchange(second.astype(jnp.float16))
    own, core, half, cross, turned = turn(first.astype(jnp.float32), second.astype(jnp.float32))

    last = tiles([up3, down3], [down1, core1, half1, cross1], [(0, 0), (0, 1), (1, 2), (1, 3)], ncol)
    last = exchange(jnp.concatenate([last, turned], axis=2))
    opposite, turned = last[:, :, : 4 * rows].sum(0), last[:, :, 4 * rows :]

    home = [
        shift(own, dz=-1),
        shift(core, dz=-1, dc=1),
        shift(half, dz=1, dy=1),
        shift(cross, dz=1, dy=1, dc=1),
    ]
    home_labels = [(k, d if k < 2 else -d) for k in range(4) for d in range(4)]
    still, above1, below1, above2, below2 = settle(turned)
    away = [
        still,
        shift(above1, dz=1),
        shift(below1, dz=-1),
        shift(above2, dz=2),
        shift(below2, dz=-2),
        shift(opposite[:, : 2 * rows], dz=3),
        shift(opposite[:, 2 * rows :], dz=-3),
    ]
    away_labels = [(0, -1), (1, -1), (2, 1), (3, 1), (0, -2), (1, -2), (2, 2), (3, 2), (0, -3), (1, -3), (2, 3), (3, 3)]
    away_labels += [(k, 4) for k in range(4)]
    return arrange(home + away, home_labels + away_labels, myself, part, rows)


def solution(mesh):
    return jax.shard_map(
        per_device,
        mesh=mesh,
        in_specs=(P("row", "col"),),
        out_specs=P(("row", "col"), None),
        check_vma=False,
    )
```

```python
import jax
import jax.numpy as jnp
from jax import lax
from jax.experimental import pallas as pl
from jax.experimental.pallas import tpu as pltpu
from jax.sharding import PartitionSpec as P

NCOL = 14336
NZ = 8
LIMIT = 60000.0
LANES = 128
SPLIT = 8193.0
VMEM = pl.BlockSpec(memory_space=pltpu.VMEM)
ROOM = pltpu.CompilerParams(vmem_limit_bytes=14 << 20)


def shift(value, dz=0, dy=0, dc=0):
    pairs = []
    for z in range(NZ):
        for y in range(2):
            for c in range(2):
                pairs.append(((z * 2 + y) * 2 + c, ((z + dz) % NZ * 2 + (y ^ dy)) * 2 + (c ^ dc)))
    return lax.ppermute(value, "row", pairs)


def hold(value, *until):
    for other in until:
        corner = other[(slice(0, 1),) * other.ndim].reshape(1, 1)
        value = value + (corner * 0).astype(value.dtype)
    return value


def tiles_kernel(nrows, ncols, pairs, scaled, *refs):
    lefts, rights, out_ref = refs[:nrows], refs[nrows : nrows + ncols], refs[-1]
    ndest, part, full = out_ref.shape
    width = rights[0].shape[0]
    most = None
    for at, (left, right) in enumerate(pairs):
        tile = lax.dot_general(
            lefts[left][...], rights[right][...], (((1,), (1,)), ((), ())), preferred_element_type=jnp.float32
        )
        out_ref[:, :, at * width : (at + 1) * width] = tile.reshape(ndest, part, width)
        most = jnp.abs(tile) if most is None else jnp.maximum(most, jnp.abs(tile))
    if scaled:
        most = jnp.max(jnp.max(most, axis=0, keepdims=True), axis=1, keepdims=True)
        power = power_of(most)
        factor = jnp.exp2(power) / (1.0 + lax.axis_index("col").astype(jnp.float32) / ndest)
        for at in range(len(pairs)):
            cut = slice(at * width, (at + 1) * width)
            out_ref[:, :, cut] = out_ref[:, :, cut] * factor.reshape(1, 1, 1)
        out_ref[:, :, full - LANES :] = jnp.broadcast_to(power.reshape(1, 1, 1), (ndest, part, LANES))


def tiles(lefts, rights, pairs, ndest, scaled=False, weigh=1):
    rows, depth = lefts[0].shape
    width = rows * len(pairs)
    return pl.pallas_call(
        lambda *refs: tiles_kernel(len(lefts), len(rights), pairs, scaled, *refs),
        in_specs=[VMEM] * (len(lefts) + len(rights)),
        out_specs=VMEM,
        out_shape=jax.ShapeDtypeStruct((ndest, rows // ndest, width + scaled * LANES), jnp.float32),
        compiler_params=ROOM,
        cost_estimate=pl.CostEstimate(
            flops=2 * rows * width * depth * weigh,
            bytes_accessed=2 * rows * depth * (len(lefts) + len(rights)) + 4 * rows * width,
            transcendentals=0,
        ),
    )(*lefts, *rights)


def power_of(most):
    return jnp.floor(jnp.log2(LIMIT / jnp.maximum(most, 1e-33)))


def summed(ref, first, count, powers):
    ndest, part, _ = ref.shape
    width = ndest * part
    weights = [
        jnp.exp2(-ref[source, :, powers : powers + 1]) * (1.0 + source / ndest) for source in range(ndest)
    ]
    sums = []
    for at in range(count):
        cut = slice(first + at * width, first + (at + 1) * width)
        value = ref[0, :, cut] * weights[0]
        for source in range(1, ndest):
            value += ref[source, :, cut] * weights[source]
        sums.append(value)
    return sums


def turn_kernel(first_ref, second_ref, last_ref, own_ref, core_ref, half_ref, cross_ref, out_ref):
    ndest, part, ahead = last_ref.shape
    width = ndest * part
    first = summed(first_ref, 0, 6, 6 * width)
    second = summed(second_ref, 0, 10, 10 * width)
    for ref, blocks in (
        (own_ref, first[:3] + second[:1]),
        (core_ref, first[3:] + second[1:2]),
        (half_ref, second[2:6]),
        (cross_ref, second[6:]),
    ):
        for at, block in enumerate(blocks):
            ref[:, at * width : (at + 1) * width] = block
    out_ref[:, :, :ahead] = last_ref[...]
    groups = (
        (first[1], first[4], second[3], second[7]),
        (first[2], first[5], second[4], second[8]),
        (second[0], second[1], second[5], second[9]),
    )
    groups = [jnp.concatenate(group, axis=0) for group in groups]
    most = jnp.maximum(jnp.maximum(jnp.abs(groups[0]), jnp.abs(groups[1])), jnp.abs(groups[2]))
    power = power_of(jnp.max(jnp.max(most, axis=0, keepdims=True), axis=1, keepdims=True))
    step = 4 * part
    for at, group in enumerate(groups):
        turned = group.T * jnp.exp2(power)
        over = turned * SPLIT
        high = over - (over - turned)
        for start, piece in ((ahead, high), (ahead + 3 * step, turned - high)):
            out_ref[:, :, start + at * step : start + (at + 1) * step] = piece.reshape(ndest, part, step)
    out_ref[:, :, ahead + 6 * step :] = jnp.broadcast_to(power.reshape(1, 1, 1), (ndest, part, LANES))


def turn(first, second, last):
    ndest, part, ahead = last.shape
    width = ndest * part
    bundle = jax.ShapeDtypeStruct((part, 4 * width), jnp.float32)
    return pl.pallas_call(
        turn_kernel,
        in_specs=[VMEM] * 3,
        out_specs=[VMEM] * 5,
        out_shape=[bundle] * 4 + [jax.ShapeDtypeStruct((ndest, part, ahead + 24 * part + LANES), jnp.float32)],
        compiler_params=ROOM,
    )(first, second, last)


def settle_kernel(in_ref, *outs):
    nsource, part, full = in_ref.shape
    width = nsource * part
    ahead = 4 * width + LANES
    opposite = summed(in_ref, 0, 4, 4 * width)
    step = 4 * part
    blocks = []
    pieces = []
    for source in range(nsource):
        weight = jnp.exp2(-in_ref[source, :, full - LANES : full - LANES + 1])
        high = in_ref[source, :, ahead : ahead + 3 * step]
        low = in_ref[source, :, ahead + 3 * step : ahead + 6 * step]
        pieces.append((high + low) * weight)
    for place in range(12):
        cut = slice(place * part, (place + 1) * part)
        blocks.append(jnp.concatenate([piece[:, cut] for piece in pieces], axis=1))
    blocks += opposite
    for ref in outs:
        for at in range(ref.shape[1] // width):
            ref[:, at * width : (at + 1) * width] = blocks.pop(0)


def settle(turned):
    nsource, part, _ = turned.shape
    width = nsource * part
    return pl.pallas_call(
        settle_kernel,
        in_specs=[VMEM],
        out_specs=[VMEM] * 7,
        out_shape=[jax.ShapeDtypeStruct((part, count * width), jnp.float32) for count in (4, 2, 2, 2, 2, 2, 2)],
        compiler_params=ROOM,
    )(turned)


def arrange_kernel(to_ref, *refs):
    blocks, out_ref = refs[:-1], refs[-1]
    place = 0
    width = out_ref.shape[1] // 32
    for ref in blocks:
        for at in range(ref.shape[1] // width):
            start = pl.multiple_of(to_ref[place] * width, width)
            out_ref[:, pl.ds(start, width)] = ref[:, at * width : (at + 1) * width] * (1.0 / NCOL)
            place += 1


def arrange(blocks, labels, myself, rows, width):
    z, mine = myself // 4, myself % 4
    rel = jnp.array([k for k, _ in labels], jnp.int32)
    slab = jnp.array([d for _, d in labels], jnp.int32)
    to = ((z + slab) % NZ * 4 + (rel ^ mine)).astype(jnp.int32)
    return pl.pallas_call(
        arrange_kernel,
        grid_spec=pltpu.PrefetchScalarGridSpec(
            num_scalar_prefetch=1, grid=(), in_specs=[VMEM] * len(blocks), out_specs=VMEM
        ),
        out_shape=jax.ShapeDtypeStruct((rows, 32 * width), jnp.float32),
        compiler_params=ROOM,
    )(to, *blocks)


def per_device(gradient):
    rows = gradient.shape[0]
    ncol = lax.axis_size("col")
    part = rows // ncol
    myself = lax.axis_index("row")

    def exchange(parts):
        return lax.all_to_all(parts, "col", 0, 0, tiled=True)

    up1, down1 = shift(gradient, dz=-1), shift(gradient, dz=1)
    half1 = shift(up1, dy=1)
    core1 = shift(hold(down1, up1), dc=1)
    up2, down2 = shift(up1, dz=-1), shift(down1, dz=1)

    near = [(row, column) for row in range(2) for column in range(3)]
    first = tiles([down1, core1], [down1, gradient, up1], near, ncol, scaled=True)
    first = exchange(first.astype(jnp.float16))
    half1 = hold(half1, first, up2, down2)
    cross1 = shift(half1, dc=1)
    up3, down3 = shift(up2, dz=-1), shift(down2, dz=1)
    middle = [(0, 0), (1, 0)] + [(row, column) for row in (2, 3) for column in (1, 2, 3, 4)]
    second = tiles([down1, core1, half1, cross1], [up2, up1, gradient, down1, down2], middle, ncol, scaled=True)
    second = exchange(second.astype(jnp.float16))
    last = tiles([up3, down3], [down1, core1, half1, cross1], [(0, 0), (0, 1), (1, 2), (1, 3)], ncol, scaled=True, weigh=40)
    own, core, half, cross, last = turn(first.astype(jnp.float32), second.astype(jnp.float32), last)
    last = exchange(last.astype(jnp.float16))

    home = [
        shift(own, dz=-1),
        shift(core, dz=-1, dc=1),
        shift(half, dz=1, dy=1),
        shift(cross, dz=1, dy=1, dc=1),
    ]
    home_labels = [(k, d if k < 2 else -d) for k in range(4) for d in range(4)]
    still, above1, below1, above2, below2, above3, below3 = settle(last.astype(jnp.float32))
    away = [
        still,
        shift(above1, dz=1),
        shift(below1, dz=-1),
        shift(above2, dz=2),
        shift(below2, dz=-2),
        shift(above3, dz=3),
        shift(below3, dz=-3),
    ]
    away_labels = [(0, -1), (1, -1), (2, 1), (3, 1), (0, -2), (1, -2), (2, 2), (3, 2), (0, -3), (1, -3), (2, 3), (3, 3)]
    away_labels += [(k, 4) for k in range(4)]
    return arrange(home + away, home_labels + away_labels, myself, part, rows)


def solution(mesh):
    return jax.shard_map(
        per_device,
        mesh=mesh,
        in_specs=(P("row", "col"),),
        out_specs=P(("row", "col"), None),
        check_vma=False,
    )
```

```python
import jax
import jax.numpy as jnp
from jax import lax
from jax.experimental import pallas as pl
from jax.experimental.pallas import tpu as pltpu
from jax.sharding import PartitionSpec as P

NCOL = 14336
NZ = 8
LIMIT = 60000.0
LANES = 128
SPLIT = 8193.0
VMEM = pl.BlockSpec(memory_space=pltpu.VMEM)
ROOM = pltpu.CompilerParams(vmem_limit_bytes=14 << 20)


def shift(value, dz=0, dy=0, dc=0):
    pairs = []
    for z in range(NZ):
        for y in range(2):
            for c in range(2):
                pairs.append(((z * 2 + y) * 2 + c, ((z + dz) % NZ * 2 + (y ^ dy)) * 2 + (c ^ dc)))
    return lax.ppermute(value, "row", pairs)


def hold(value, *until):
    for other in until:
        corner = other[(slice(0, 1),) * other.ndim].reshape(1, 1)
        value = value + (corner * 0).astype(value.dtype)
    return value


def tiles_kernel(nrows, ncols, pairs, scaled, *refs):
    lefts, rights, out_ref = refs[:nrows], refs[nrows : nrows + ncols], refs[-1]
    ndest, part, full = out_ref.shape
    width = rights[0].shape[0]
    most = None
    for at, (left, right) in enumerate(pairs):
        tile = lax.dot_general(
            lefts[left][...], rights[right][...], (((1,), (1,)), ((), ())), preferred_element_type=jnp.float32
        )
        out_ref[:, :, at * width : (at + 1) * width] = tile.reshape(ndest, part, width)
        most = jnp.abs(tile) if most is None else jnp.maximum(most, jnp.abs(tile))
    if scaled:
        most = jnp.max(jnp.max(most, axis=0, keepdims=True), axis=1, keepdims=True)
        power = power_of(most)
        factor = jnp.exp2(power) / (1.0 + lax.axis_index("col").astype(jnp.float32) / ndest)
        for at in range(len(pairs)):
            cut = slice(at * width, (at + 1) * width)
            out_ref[:, :, cut] = out_ref[:, :, cut] * factor.reshape(1, 1, 1)
        out_ref[:, :, full - LANES :] = jnp.broadcast_to(power.reshape(1, 1, 1), (ndest, part, LANES))


def tiles(lefts, rights, pairs, ndest, scaled=False, weigh=1):
    rows, depth = lefts[0].shape
    width = rows * len(pairs)
    return pl.pallas_call(
        lambda *refs: tiles_kernel(len(lefts), len(rights), pairs, scaled, *refs),
        in_specs=[VMEM] * (len(lefts) + len(rights)),
        out_specs=VMEM,
        out_shape=jax.ShapeDtypeStruct((ndest, rows // ndest, width + scaled * LANES), jnp.float32),
        compiler_params=ROOM,
        cost_estimate=pl.CostEstimate(
            flops=2 * rows * width * depth * weigh,
            bytes_accessed=2 * rows * depth * (len(lefts) + len(rights)) + 4 * rows * width,
            transcendentals=0,
        ),
    )(*lefts, *rights)


def power_of(most):
    return jnp.floor(jnp.log2(LIMIT / jnp.maximum(most, 1e-33)))


def summed(ref, first, count, powers):
    ndest, part, _ = ref.shape
    width = ndest * part
    weights = [
        jnp.exp2(-ref[source, :, powers : powers + 1]) * (1.0 + source / ndest) for source in range(ndest)
    ]
    sums = []
    for at in range(count):
        cut = slice(first + at * width, first + (at + 1) * width)
        value = ref[0, :, cut] * weights[0]
        for source in range(1, ndest):
            value += ref[source, :, cut] * weights[source]
        sums.append(value)
    return sums


def turn_kernel(first_ref, second_ref, last_ref, own_ref, core_ref, half_ref, cross_ref, out_ref):
    ndest, part, ahead = last_ref.shape
    width = ndest * part
    first = summed(first_ref, 0, 6, 6 * width)
    second = summed(second_ref, 0, 10, 10 * width)
    for ref, blocks in (
        (own_ref, first[:3] + second[:1]),
        (core_ref, first[3:] + second[1:2]),
        (half_ref, second[2:6]),
        (cross_ref, second[6:]),
    ):
        for at, block in enumerate(blocks):
            ref[:, at * width : (at + 1) * width] = block
    out_ref[:, :, :ahead] = last_ref[...]
    groups = (
        (first[1], first[4], second[3], second[7]),
        (first[2], first[5], second[4], second[8]),
        (second[0], second[1], second[5], second[9]),
    )
    groups = [jnp.concatenate(group, axis=0) for group in groups]
    most = jnp.maximum(jnp.maximum(jnp.abs(groups[0]), jnp.abs(groups[1])), jnp.abs(groups[2]))
    power = power_of(jnp.max(jnp.max(most, axis=0, keepdims=True), axis=1, keepdims=True))
    step = 4 * part
    for at, group in enumerate(groups):
        turned = group.T * jnp.exp2(power)
        over = turned * SPLIT
        high = over - (over - turned)
        for start, piece in ((ahead, high), (ahead + 3 * step, turned - high)):
            out_ref[:, :, start + at * step : start + (at + 1) * step] = piece.reshape(ndest, part, step)
    out_ref[:, :, ahead + 6 * step :] = jnp.broadcast_to(power.reshape(1, 1, 1), (ndest, part, LANES))


def turn(first, second, last):
    ndest, part, ahead = last.shape
    width = ndest * part
    bundle = jax.ShapeDtypeStruct((part, 4 * width), jnp.float32)
    return pl.pallas_call(
        turn_kernel,
        in_specs=[VMEM] * 3,
        out_specs=[VMEM] * 5,
        out_shape=[bundle] * 4 + [jax.ShapeDtypeStruct((ndest, part, ahead + 24 * part + LANES), jnp.float32)],
        compiler_params=ROOM,
    )(first, second, last)


def settle_kernel(in_ref, *outs):
    nsource, part, full = in_ref.shape
    width = nsource * part
    ahead = 4 * width + LANES
    opposite = summed(in_ref, 0, 4, 4 * width)
    step = 4 * part
    blocks = []
    pieces = []
    for source in range(nsource):
        weight = jnp.exp2(-in_ref[source, :, full - LANES : full - LANES + 1])
        high = in_ref[source, :, ahead : ahead + 3 * step]
        low = in_ref[source, :, ahead + 3 * step : ahead + 6 * step]
        pieces.append((high + low) * weight)
    for place in range(12):
        cut = slice(place * part, (place + 1) * part)
        blocks.append(jnp.concatenate([piece[:, cut] for piece in pieces], axis=1))
    blocks += opposite
    for ref in outs:
        for at in range(ref.shape[1] // width):
            ref[:, at * width : (at + 1) * width] = blocks.pop(0)


def settle(turned):
    nsource, part, _ = turned.shape
    width = nsource * part
    return pl.pallas_call(
        settle_kernel,
        in_specs=[VMEM],
        out_specs=[VMEM] * 7,
        out_shape=[jax.ShapeDtypeStruct((part, count * width), jnp.float32) for count in (4, 2, 2, 2, 2, 2, 2)],
        compiler_params=ROOM,
    )(turned)


def arrange_kernel(to_ref, *refs):
    blocks, out_ref = refs[:-1], refs[-1]
    place = 0
    width = out_ref.shape[1] // 32
    for ref in blocks:
        for at in range(ref.shape[1] // width):
            start = pl.multiple_of(to_ref[place] * width, width)
            out_ref[:, pl.ds(start, width)] = ref[:, at * width : (at + 1) * width] * (1.0 / NCOL)
            place += 1


def arrange(blocks, labels, myself, rows, width):
    z, mine = myself // 4, myself % 4
    rel = jnp.array([k for k, _ in labels], jnp.int32)
    slab = jnp.array([d for _, d in labels], jnp.int32)
    to = ((z + slab) % NZ * 4 + (rel ^ mine)).astype(jnp.int32)
    return pl.pallas_call(
        arrange_kernel,
        grid_spec=pltpu.PrefetchScalarGridSpec(
            num_scalar_prefetch=1, grid=(), in_specs=[VMEM] * len(blocks), out_specs=VMEM
        ),
        out_shape=jax.ShapeDtypeStruct((rows, 32 * width), jnp.float32),
        compiler_params=ROOM,
    )(to, *blocks)


def per_device(gradient):
    rows = gradient.shape[0]
    ncol = lax.axis_size("col")
    part = rows // ncol
    myself = lax.axis_index("row")

    def exchange(parts):
        return lax.all_to_all(parts, "col", 0, 0, tiled=True)

    up1, down1 = shift(gradient, dz=-1), shift(gradient, dz=1)
    half1 = shift(up1, dy=1)
    core1 = shift(down1, dc=1)
    up2, down2 = shift(up1, dz=-1), shift(down1, dz=1)

    near = [(row, column) for row in range(2) for column in range(3)]
    first = tiles([down1, core1], [down1, gradient, up1], near, ncol, scaled=True)
    first = exchange(first.astype(jnp.float16))
    half1 = hold(half1, first)
    cross1 = shift(half1, dc=1)
    up3, down3 = shift(up2, dz=-1), shift(down2, dz=1)
    middle = [(0, 0), (1, 0)] + [(row, column) for row in (2, 3) for column in (1, 2, 3, 4)]
    second = tiles([down1, core1, half1, cross1], [up2, up1, gradient, down1, down2], middle, ncol, scaled=True)
    second = exchange(second.astype(jnp.float16))
    last = tiles([up3, down3], [down1, core1, half1, cross1], [(0, 0), (0, 1), (1, 2), (1, 3)], ncol, scaled=True, weigh=40)
    own, core, half, cross, last = turn(first.astype(jnp.float32), second.astype(jnp.float32), last)
    last = exchange(last.astype(jnp.float16))

    home = [
        shift(own, dz=-1),
        shift(core, dz=-1, dc=1),
        shift(half, dz=1, dy=1),
        shift(cross, dz=1, dy=1, dc=1),
    ]
    home_labels = [(k, d if k < 2 else -d) for k in range(4) for d in range(4)]
    still, above1, below1, above2, below2, above3, below3 = settle(last.astype(jnp.float32))
    away = [
        still,
        shift(above1, dz=1),
        shift(below1, dz=-1),
        shift(above2, dz=2),
        shift(below2, dz=-2),
        shift(above3, dz=3),
        shift(below3, dz=-3),
    ]
    away_labels = [(0, -1), (1, -1), (2, 1), (3, 1), (0, -2), (1, -2), (2, 2), (3, 2), (0, -3), (1, -3), (2, 3), (3, 3)]
    away_labels += [(k, 4) for k in range(4)]
    return arrange(home + away, home_labels + away_labels, myself, part, rows)


def solution(mesh):
    return jax.shard_map(
        per_device,
        mesh=mesh,
        in_specs=(P("row", "col"),),
        out_specs=P(("row", "col"), None),
        check_vma=False,
    )
```

```python
import jax
import jax.numpy as jnp
from jax import lax
from jax.experimental import pallas as pl
from jax.experimental.pallas import tpu as pltpu
from jax.sharding import PartitionSpec as P

NCOL = 14336
NZ = 8
LIMIT = 60000.0
LANES = 128
SPLIT = 8193.0
VMEM = pl.BlockSpec(memory_space=pltpu.VMEM)
ROOM = pltpu.CompilerParams(vmem_limit_bytes=14 << 20)


def shift(value, dz=0, dy=0, dc=0):
    pairs = []
    for z in range(NZ):
        for y in range(2):
            for c in range(2):
                pairs.append(((z * 2 + y) * 2 + c, ((z + dz) % NZ * 2 + (y ^ dy)) * 2 + (c ^ dc)))
    return lax.ppermute(value, "row", pairs)


def hold(value, *until):
    for other in until:
        corner = other[(slice(0, 1),) * other.ndim].reshape(1, 1)
        value = value + (corner * 0).astype(value.dtype)
    return value


def tiles_kernel(nrows, ncols, pairs, scaled, *refs):
    lefts, rights, out_ref = refs[:nrows], refs[nrows : nrows + ncols], refs[-1]
    ndest, part, full = out_ref.shape
    width = rights[0].shape[0]
    most = None
    for at, (left, right) in enumerate(pairs):
        tile = lax.dot_general(
            lefts[left][...], rights[right][...], (((1,), (1,)), ((), ())), preferred_element_type=jnp.float32
        )
        out_ref[:, :, at * width : (at + 1) * width] = tile.reshape(ndest, part, width)
        most = jnp.abs(tile) if most is None else jnp.maximum(most, jnp.abs(tile))
    if scaled:
        most = jnp.max(jnp.max(most, axis=0, keepdims=True), axis=1, keepdims=True)
        power = power_of(most)
        factor = jnp.exp2(power) / (1.0 + lax.axis_index("col").astype(jnp.float32) / ndest)
        for at in range(len(pairs)):
            cut = slice(at * width, (at + 1) * width)
            out_ref[:, :, cut] = out_ref[:, :, cut] * factor.reshape(1, 1, 1)
        out_ref[:, :, full - LANES :] = jnp.broadcast_to(power.reshape(1, 1, 1), (ndest, part, LANES))


def tiles(lefts, rights, pairs, ndest, scaled=False, weigh=1):
    rows, depth = lefts[0].shape
    width = rows * len(pairs)
    return pl.pallas_call(
        lambda *refs: tiles_kernel(len(lefts), len(rights), pairs, scaled, *refs),
        in_specs=[VMEM] * (len(lefts) + len(rights)),
        out_specs=VMEM,
        out_shape=jax.ShapeDtypeStruct((ndest, rows // ndest, width + scaled * LANES), jnp.float32),
        compiler_params=ROOM,
        cost_estimate=pl.CostEstimate(
            flops=2 * rows * width * depth * weigh,
            bytes_accessed=2 * rows * depth * (len(lefts) + len(rights)) + 4 * rows * width,
            transcendentals=0,
        ),
    )(*lefts, *rights)


def power_of(most):
    return jnp.floor(jnp.log2(LIMIT / jnp.maximum(most, 1e-33)))


def summed(ref, first, count, powers):
    ndest, part, _ = ref.shape
    width = ndest * part
    weights = [
        jnp.exp2(-ref[source, :, powers : powers + 1]) * (1.0 + source / ndest) for source in range(ndest)
    ]
    sums = []
    for at in range(count):
        cut = slice(first + at * width, first + (at + 1) * width)
        value = ref[0, :, cut] * weights[0]
        for source in range(1, ndest):
            value += ref[source, :, cut] * weights[source]
        sums.append(value)
    return sums


def turn_kernel(zero_ref, first_ref, second_ref, last_ref, own_ref, core_ref, half_ref, cross_ref, diagonal_ref, side_ref, out_ref):
    ndest, part, ahead = last_ref.shape
    width = ndest * part
    zero = summed(zero_ref, 0, 2, 2 * width)
    first = summed(first_ref, 0, 4, 4 * width)
    second = summed(second_ref, 0, 10, 10 * width)
    for ref, blocks in (
        (own_ref, first[:2] + second[:1]),
        (core_ref, first[2:] + second[1:2]),
        (half_ref, second[2:6]),
        (cross_ref, second[6:]),
        (diagonal_ref, zero[:1]),
        (side_ref, zero[1:]),
    ):
        for at, block in enumerate(blocks):
            ref[:, at * width : (at + 1) * width] = block
    out_ref[:, :, :ahead] = last_ref[...]
    groups = (
        (first[0], first[2], second[3], second[7]),
        (first[1], first[3], second[4], second[8]),
        (second[0], second[1], second[5], second[9]),
    )
    groups = [jnp.concatenate(group, axis=0) for group in groups]
    most = jnp.maximum(jnp.maximum(jnp.abs(groups[0]), jnp.abs(groups[1])), jnp.abs(groups[2]))
    power = power_of(jnp.max(jnp.max(most, axis=0, keepdims=True), axis=1, keepdims=True))
    step = 4 * part
    for at, group in enumerate(groups):
        turned = group.T * jnp.exp2(power)
        over = turned * SPLIT
        high = over - (over - turned)
        for start, piece in ((ahead, high), (ahead + 3 * step, turned - high)):
            out_ref[:, :, start + at * step : start + (at + 1) * step] = piece.reshape(ndest, part, step)
    out_ref[:, :, ahead + 6 * step :] = jnp.broadcast_to(power.reshape(1, 1, 1), (ndest, part, LANES))


def turn(zero, first, second, last):
    ndest, part, ahead = last.shape
    width = ndest * part
    bundles = [jax.ShapeDtypeStruct((part, count * width), jnp.float32) for count in (3, 3, 4, 4, 1, 1)]
    return pl.pallas_call(
        turn_kernel,
        in_specs=[VMEM] * 4,
        out_specs=[VMEM] * 7,
        out_shape=bundles + [jax.ShapeDtypeStruct((ndest, part, ahead + 24 * part + LANES), jnp.float32)],
        compiler_params=ROOM,
    )(zero, first, second, last)


def settle_kernel(in_ref, *outs):
    nsource, part, full = in_ref.shape
    width = nsource * part
    ahead = 4 * width + LANES
    opposite = summed(in_ref, 0, 4, 4 * width)
    step = 4 * part
    blocks = []
    pieces = []
    for source in range(nsource):
        weight = jnp.exp2(-in_ref[source, :, full - LANES : full - LANES + 1])
        high = in_ref[source, :, ahead : ahead + 3 * step]
        low = in_ref[source, :, ahead + 3 * step : ahead + 6 * step]
        pieces.append((high + low) * weight)
    for place in range(12):
        cut = slice(place * part, (place + 1) * part)
        blocks.append(jnp.concatenate([piece[:, cut] for piece in pieces], axis=1))
    blocks += opposite
    for ref in outs:
        for at in range(ref.shape[1] // width):
            ref[:, at * width : (at + 1) * width] = blocks.pop(0)


def settle(turned):
    nsource, part, _ = turned.shape
    width = nsource * part
    return pl.pallas_call(
        settle_kernel,
        in_specs=[VMEM],
        out_specs=[VMEM] * 7,
        out_shape=[jax.ShapeDtypeStruct((part, count * width), jnp.float32) for count in (4, 2, 2, 2, 2, 2, 2)],
        compiler_params=ROOM,
    )(turned)


def arrange_kernel(to_ref, *refs):
    blocks, out_ref = refs[:-1], refs[-1]
    place = 0
    width = out_ref.shape[1] // 32
    for ref in blocks:
        for at in range(ref.shape[1] // width):
            start = pl.multiple_of(to_ref[place] * width, width)
            out_ref[:, pl.ds(start, width)] = ref[:, at * width : (at + 1) * width] * (1.0 / NCOL)
            place += 1


def arrange(blocks, labels, myself, rows, width):
    z, mine = myself // 4, myself % 4
    rel = jnp.array([k for k, _ in labels], jnp.int32)
    slab = jnp.array([d for _, d in labels], jnp.int32)
    to = ((z + slab) % NZ * 4 + (rel ^ mine)).astype(jnp.int32)
    return pl.pallas_call(
        arrange_kernel,
        grid_spec=pltpu.PrefetchScalarGridSpec(
            num_scalar_prefetch=1, grid=(), in_specs=[VMEM] * len(blocks), out_specs=VMEM
        ),
        out_shape=jax.ShapeDtypeStruct((rows, 32 * width), jnp.float32),
        compiler_params=ROOM,
    )(to, *blocks)


def per_device(gradient):
    rows = gradient.shape[0]
    ncol = lax.axis_size("col")
    part = rows // ncol
    myself = lax.axis_index("row")

    def exchange(parts):
        return lax.all_to_all(parts, "col", 0, 0, tiled=True)

    up1, down1 = shift(gradient, dz=-1), shift(gradient, dz=1)
    core0 = shift(gradient, dc=1)
    zero = tiles([gradient, core0], [gradient], [(0, 0), (1, 0)], ncol, scaled=True)
    zero = exchange(zero.astype(jnp.float16))
    half1 = shift(up1, dy=1)
    core1 = shift(hold(down1, zero, up1), dc=1)
    up2, down2 = shift(up1, dz=-1), shift(down1, dz=1)

    near = [(row, column) for row in range(2) for column in range(2)]
    first = tiles([down1, core1], [gradient, up1], near, ncol, scaled=True)
    first = exchange(first.astype(jnp.float16))
    half1 = hold(half1, first)
    cross1 = shift(half1, dc=1)
    up3, down3 = shift(up2, dz=-1), shift(down2, dz=1)
    middle = [(0, 0), (1, 0)] + [(row, column) for row in (2, 3) for column in (1, 2, 3, 4)]
    second = tiles([down1, core1, half1, cross1], [up2, up1, gradient, down1, down2], middle, ncol, scaled=True)
    second = exchange(second.astype(jnp.float16))
    last = tiles([up3, down3], [down1, core1, half1, cross1], [(0, 0), (0, 1), (1, 2), (1, 3)], ncol, scaled=True, weigh=40)
    own, core, half, cross, diagonal, side, last = turn(
        zero.astype(jnp.float32), first.astype(jnp.float32), second.astype(jnp.float32), last
    )
    last = exchange(last.astype(jnp.float16))

    home = [
        shift(own, dz=-1),
        shift(core, dz=-1, dc=1),
        shift(half, dz=1, dy=1),
        shift(cross, dz=1, dy=1, dc=1),
        diagonal,
        shift(side, dc=1),
    ]
    home_labels = [(k, d) for k in range(2) for d in range(1, 4)] + [(k, -d) for k in (2, 3) for d in range(4)]
    home_labels += [(0, 0), (1, 0)]
    still, above1, below1, above2, below2, above3, below3 = settle(last.astype(jnp.float32))
    away = [
        still,
        shift(above1, dz=1),
        shift(below1, dz=-1),
        shift(above2, dz=2),
        shift(below2, dz=-2),
        shift(above3, dz=3),
        shift(below3, dz=-3),
    ]
    away_labels = [(0, -1), (1, -1), (2, 1), (3, 1), (0, -2), (1, -2), (2, 2), (3, 2), (0, -3), (1, -3), (2, 3), (3, 3)]
    away_labels += [(k, 4) for k in range(4)]
    return arrange(home + away, home_labels + away_labels, myself, part, rows)


def solution(mesh):
    return jax.shard_map(
        per_device,
        mesh=mesh,
        in_specs=(P("row", "col"),),
        out_specs=P(("row", "col"), None),
        check_vma=False,
    )
```
